32 devices in a mesh: design: 2 (over y), harm: 4 (over z), tile: 4 (over x, core).
Axes of the slice: x: 2, y: 2, z: 4, core: 2. Of those that a mesh axis runs over, the one named last changes fastest.
Arguments:
- fwd_ckpt: bfloat16 [8, 2, 2, 6, 3, 2624], P(('design', 'tile'), None, None, None, None, 'harm'), parts along dimension 0, as said below
- adj_amp: bfloat16 [4, 2, 6, 3, 2624], P('design', None, None, None, 'harm'), parts along dimension 0, as said below
- layer_owner: int32 [4], P('design'), parts along dimension 0, may hold values from 0 to 3, as said below
- source_list: int32 [12], P('design'), parts along dimension 0, may hold values from 0 to 5, each once
Outputs:
- grad: float32 [4, 8192], P('design', ('harm', 'tile')), parts along dimension 0
The draws below stay inside these ranges and needn't reach their ends.
There are 2 independent parts, one for each index of `design`. The reference program is written for one: setup_inputs(seed, part) draws one part's arguments, and reference() takes and returns one part's arrays. A program takes and returns all parts, laid end to end along the dimension named above; each array names one. Nothing has to cross between parts.
Inputs may be any that keep to these rules, and one draw needn't show every extreme that they name: `layer_owner`: the layers' slots are distinct. `source_list`: each source appears once. `fwd_ckpt`: entries of harmonics 2601 and above are zero. `adj_amp`: entries of harmonics 2601 and above are zero.
All inputs are finite; a program needn't handle non-finite values.
Results may differ from the reference program's by a relative error of at most 0.0034.
Values may be sent and summed in bfloat16 or wider, within the bound.
A program may use at most 64 MiB of HBM per device.

```python
import math
import jax
import jax.numpy as jnp
from jax import lax

GRID = 512
ORD = 51
H = 2624
L = 2
S = 6
PIX_DEV = 512
R = 18
SLOTS = 4
NPIX = 8192
N_TILE = 4


def draw_layer_owner(key, part):
    return jax.random.permutation(key, SLOTS)[:L].astype(jnp.int32)


def masked_amplitudes(key, shape):
    scale = (2.0 * H) ** (-0.5)
    values = jax.random.truncated_normal(jax.random.fold_in(key, 13), -6.0, 6.0, shape, jnp.float32)
    harmonic = jnp.arange(H, dtype=jnp.int32)
    keep = (harmonic < ORD * ORD).astype(jnp.float32)
    return (values * scale * keep).astype(jnp.bfloat16)


def draw_fwd_ckpt(key, part):
    return masked_amplitudes(key, (SLOTS, L, 2, S, 3, H))


def draw_adj_amp(key, part):
    return masked_amplitudes(key, (L, 2, S, 3, H))


def setup_inputs(seed: int = 0, part: int = 0) -> dict:
    arg_keys = jax.random.split(jax.random.key(seed), 5)
    part_splits = jax.random.split(jax.random.fold_in(arg_keys[4], part), 5)
    return {
        "fwd_ckpt": draw_fwd_ckpt(jax.random.fold_in(jax.random.fold_in(arg_keys[4], part), 71), part),
        "adj_amp": draw_adj_amp(jax.random.fold_in(jax.random.fold_in(arg_keys[4], part), 71), part),
        "layer_owner": draw_layer_owner(jax.random.fold_in(jax.random.fold_in(arg_keys[4], part), 71), part),
        "source_list": jax.random.permutation(part_splits[3], S).astype(jnp.int32),
    }


def make_basis(first, count):
    harmonic = jnp.arange(H, dtype=jnp.int32)
    order_x = harmonic % ORD - ORD // 2
    order_y = harmonic // ORD - ORD // 2
    pixel = first + jnp.arange(count, dtype=jnp.int32)
    column = pixel % GRID
    row_id = pixel // GRID
    phase = jnp.mod(order_x[:, None] * column[None, :] + order_y[:, None] * row_id[None, :], GRID)
    angle = phase.astype(jnp.float32) * jnp.float32(2.0 * math.pi / GRID)
    return jnp.concatenate([jnp.cos(angle), jnp.sin(angle)], axis=0).astype(jnp.bfloat16)


def panel(amp):
    real_part = amp[:, 0].reshape(L, R, H)
    imag_part = amp[:, 1].reshape(L, R, H)
    upper = jnp.concatenate([real_part, -imag_part], axis=2)
    lower = jnp.concatenate([imag_part, real_part], axis=2)
    return jnp.concatenate([upper, lower], axis=1).reshape(L * 2 * R, 2 * H)


def reference(fwd_ckpt, adj_amp, layer_owner, source_list):
    forward = jnp.stack([fwd_ckpt[layer_owner[l], l] for l in range(L)])
    forward = jnp.take(forward, source_list, axis=2)
    fwd_panel = panel(forward)
    adj_panel = panel(adj_amp)
    block = PIX_DEV * N_TILE
    blocks = NPIX // block

    def one_block(index):
        basis = make_basis(index * block, block)
        fwd_field = jnp.dot(fwd_panel, basis, preferred_element_type=jnp.float32).reshape(L, 2, R, block)
        adj_field = jnp.dot(adj_panel, basis, preferred_element_type=jnp.float32).reshape(L, 2, R, block)
        total = jnp.sum(fwd_field[:, 0] * adj_field[:, 0], axis=1) - jnp.sum(fwd_field[:, 1] * adj_field[:, 1], axis=1)
        return total * jnp.float32(R ** -0.5)

    result = lax.map(one_block, jnp.arange(blocks, dtype=jnp.int32))
    return jnp.transpose(result, (1, 0, 2)).reshape(L, NPIX)
```

```python
import functools
import math

import jax
import jax.numpy as jnp
import ml_dtypes
import numpy as np
from jax import lax
from jax.experimental import pallas as pl
from jax.experimental.pallas import tpu as pltpu
from jax.sharding import PartitionSpec as P

GRID = 512
ORD = 51
HALF = 64
LANES = 128
ROWS = 24
MESH = pl.DeviceIdType.MESH


def split(value):
    high = value.astype(ml_dtypes.bfloat16)
    low = (value - high.astype(value.dtype)).astype(ml_dtypes.bfloat16)
    return high, low


def make_tables(n_harm, n_tile, depth, wide):
    harmonic = np.arange(n_harm * depth).reshape(n_harm, depth)
    order_y = harmonic // ORD - ORD // 2
    place_x = harmonic % ORD
    row_id = np.arange(n_harm * n_tile)
    angle = (order_y[:, None, :] * row_id[None, :, None] % GRID) * (2.0 * math.pi / GRID)
    twiddle = np.zeros((n_harm, n_harm * n_tile, 2, wide), np.float32)
    twiddle[:, :, 0, :depth] = np.cos(angle)
    twiddle[:, :, 1, :depth] = np.sin(angle)
    pick = np.zeros((n_harm, wide, LANES), ml_dtypes.bfloat16)
    lane = np.arange(LANES) % HALF
    pick[:, :depth, :] = place_x[:, :, None] == lane[None, None, :]
    order_x = np.arange(ORD) - ORD // 2
    angle = (order_x[:, None] * np.arange(GRID)[None, :] % GRID) * (2.0 * math.pi / GRID)
    column = np.zeros((LANES, 2 * GRID), np.float32)
    column[:ORD, :GRID] = np.cos(angle)
    column[HALF : HALF + ORD, :GRID] = -np.sin(angle)
    column[:ORD, GRID:] = np.sin(angle)
    column[HALF : HALF + ORD, GRID:] = np.cos(angle)
    return twiddle, pick, np.stack(split(column))


def kernel(
    n_harm, n_tile, fwd_ref, adj_ref, owner_ref, source_ref, twiddle_hbm, pick_hbm, column_hbm,
    out_ref, twiddle, pick, column, amp, left, send_f, send_a, recv_f, recv_a,
    load_sem, sent_f, sent_a, got_f, got_a,
):
    layers, _, sources, comps, depth = adj_ref.shape
    n_dev = n_harm * n_tile
    wide = amp.shape[-1]
    harm = lax.axis_index("harm")
    tile = lax.axis_index("tile")
    me = harm * n_tile + tile

    loads = [
        pltpu.make_async_copy(twiddle_hbm.at[harm], twiddle, load_sem.at[0]),
        pltpu.make_async_copy(pick_hbm.at[harm], pick, load_sem.at[1]),
        pltpu.make_async_copy(column_hbm, column, load_sem.at[2]),
    ]
    for load in loads:
        load.start()

    def peer(step):
        other = lax.rem(me + step, n_dev)
        return other, {"harm": other // n_tile, "tile": lax.rem(other, n_tile)}

    barrier = pltpu.get_barrier_semaphore()

    def greet(step, carry):
        pl.semaphore_signal(barrier, inc=1, device_id=peer(step)[1], device_id_type=MESH)
        return carry

    lax.fori_loop(1, n_dev, greet, 0)

    amp[...] = jnp.zeros_like(amp)
    mine = jnp.int32(0)
    for layer in range(1, layers):
        mine = jnp.where(owner_ref[layer] == tile, layer, mine)
    for part in range(2):
        for source in range(sources):
            rows = slice(source * comps, source * comps + comps)
            amp[0, part, rows, :depth] = fwd_ref[0, mine, part, source_ref[source]].astype(jnp.float32)
            for layer in range(layers):
                amp[1 + layer, part, rows, :depth] = adj_ref[layer, part, source].astype(jnp.float32)
    loads[0].wait()
    loads[1].wait()

    low_lanes = lax.broadcasted_iota(jnp.int32, (ROWS, LANES), 1) < HALF

    def stage(group, row_id, slot):
        cosine = twiddle[row_id, 0:1, :]
        sine = twiddle[row_id, 1:2, :]
        real, imag = amp[group, 0], amp[group, 1]
        turned = jnp.concatenate(
            [real * cosine - imag * sine, real * sine + imag * cosine], axis=0
        )
        high = turned.astype(jnp.bfloat16)
        rows = slice(slot * 2 * ROWS, (slot + 1) * 2 * ROWS)
        left[0, rows, :] = high
        left[1, rows, :] = (turned - high.astype(jnp.float32)).astype(jnp.bfloat16)

    def partial_sums(to_harm):
        for to_tile in range(n_tile):
            stage(0, to_harm * n_tile + to_tile, to_tile)
        for layer in range(layers):
            stage(1 + layer, to_harm * n_tile + tile, n_tile + layer)
        right = pick[...]
        sums = jnp.dot(left[0], right, preferred_element_type=jnp.float32) + jnp.dot(
            left[1], right, preferred_element_type=jnp.float32
        )
        packed = []
        for slot in range(n_tile + layers):
            start = slot * 2 * ROWS
            packed.append(
                jnp.where(low_lanes, sums[start : start + ROWS], sums[start + ROWS : start + 2 * ROWS])
            )
        return packed[:n_tile], packed[n_tile:]

    def copy_f(to_harm, to_tile, slot):
        return pltpu.make_async_remote_copy(
            src_ref=send_f.at[to_harm * n_tile + to_tile],
            dst_ref=recv_f.at[slot],
            send_sem=sent_f.at[to_harm * n_tile + to_tile],
            recv_sem=got_f.at[slot],
            device_id={"harm": to_harm, "tile": to_tile},
            device_id_type=MESH,
        )

    def copy_a(to_harm, slot):
        return pltpu.make_async_remote_copy(
            src_ref=send_a.at[to_harm],
            dst_ref=recv_a.at[slot],
            send_sem=sent_a.at[to_harm],
            recv_sem=got_a.at[slot],
            device_id={"harm": to_harm, "tile": tile},
            device_id_type=MESH,
        )

    def compute(to_harm):
        fwd, adj = partial_sums(to_harm)
        for to_tile in range(n_tile):
            send_f[to_harm * n_tile + to_tile] = fwd[to_tile]
        send_a[to_harm] = jnp.concatenate(adj, axis=0)

    def block(step):
        to_harm = lax.rem(harm + step, n_harm)
        compute(to_harm)
        return to_harm

    def send_block(to_harm):
        for to_tile in range(n_tile):
            copy_f(to_harm, to_tile, me).start()
        copy_a(to_harm, harm).start()

    first = block(1)
    pl.semaphore_wait(barrier, n_dev - 1)
    send_block(first)

    def away(step, carry):
        send_block(block(step))
        return carry

    lax.fori_loop(2, n_harm, away, 0)

    compute(harm)
    for step in range(1, n_tile):
        copy_f(harm, lax.rem(tile + step, n_tile), me).start()
    recv_f[me] = send_f[me]
    recv_a[harm] = send_a[harm]
    loads[2].wait()

    def arrive_f(step, carry):
        other, _ = peer(step)
        copy_f(other // n_tile, lax.rem(other, n_tile), other).wait()
        return carry

    def arrive_a(step, carry):
        other = lax.rem(harm + step, n_harm)
        copy_a(other, other).wait()
        return carry

    lax.fori_loop(1, n_dev, arrive_f, 0)
    lax.fori_loop(1, n_harm, arrive_a, 0)

    def add_f(layer):
        owner = owner_ref[layer]
        return lax.fori_loop(
            0,
            n_harm,
            lambda source, total: total + recv_f[source * n_tile + owner],
            jnp.zeros((ROWS, LANES), jnp.float32),
        )

    adj = lax.fori_loop(
        0,
        n_harm,
        lambda source, total: total + recv_a[source],
        jnp.zeros((layers * ROWS, LANES), jnp.float32),
    )
    lines = jnp.concatenate([add_f(layer) for layer in range(layers)] + [adj], axis=0)
    high = lines.astype(jnp.bfloat16)
    low = (lines - high.astype(jnp.float32)).astype(jnp.bfloat16)
    fields = (
        jnp.dot(high, column[0], preferred_element_type=jnp.float32)
        + jnp.dot(low, column[0], preferred_element_type=jnp.float32)
        + jnp.dot(high, column[1], preferred_element_type=jnp.float32)
    )
    for layer in range(layers):
        one = fields[layer * ROWS : (layer + 1) * ROWS]
        two = fields[(layers + layer) * ROWS : (layers + layer + 1) * ROWS]
        both = one * two
        out_ref[layer : layer + 1, :] = jnp.sum(
            both[:, :GRID] - both[:, GRID:], axis=0, keepdims=True
        )


def per_device(n_harm, n_tile, fwd_ckpt, adj_amp, layer_owner, source_list):
    layers, _, sources, comps, depth = adj_amp.shape
    assert sources * comps <= ROWS
    wide = -(-depth // LANES) * LANES
    n_dev = n_harm * n_tile
    twiddle, pick, column = make_tables(n_harm, n_tile, depth, wide)
    slots = n_tile + layers
    vmem = pl.BlockSpec(memory_space=pltpu.VMEM)
    smem = pl.BlockSpec(memory_space=pltpu.SMEM)
    hbm = pl.BlockSpec(memory_space=pl.ANY)
    total = pl.pallas_call(
        functools.partial(kernel, n_harm, n_tile),
        out_shape=jax.ShapeDtypeStruct((layers, GRID), jnp.float32),
        in_specs=[vmem, vmem, smem, smem, hbm, hbm, hbm],
        out_specs=vmem,
        scratch_shapes=[
            pltpu.VMEM((n_dev, 2, wide), jnp.float32),
            pltpu.VMEM((wide, LANES), jnp.bfloat16),
            pltpu.VMEM(column.shape, jnp.bfloat16),
            pltpu.VMEM((1 + layers, 2, ROWS, wide), jnp.float32),
            pltpu.VMEM((2, slots * 2 * ROWS, wide), jnp.bfloat16),
            pltpu.VMEM((n_dev, ROWS, LANES), jnp.float32),
            pltpu.VMEM((n_harm, layers * ROWS, LANES), jnp.float32),
            pltpu.VMEM((n_dev, ROWS, LANES), jnp.float32),
            pltpu.VMEM((n_harm, layers * ROWS, LANES), jnp.float32),
            pltpu.SemaphoreType.DMA((3,)),
            pltpu.SemaphoreType.DMA((n_dev,)),
            pltpu.SemaphoreType.DMA((n_harm,)),
            pltpu.SemaphoreType.DMA((n_dev,)),
            pltpu.SemaphoreType.DMA((n_harm,)),
        ],
        compiler_params=pltpu.CompilerParams(
            collective_id=0, has_side_effects=True, vmem_limit_bytes=40 * 1024 * 1024
        ),
    )(
        fwd_ckpt, adj_amp, layer_owner, source_list,
        jnp.asarray(twiddle), jnp.asarray(pick), jnp.asarray(column),
    )
    return total * jnp.float32((sources * comps) ** (-0.5))


def solution(mesh):
    return jax.shard_map(
        functools.partial(per_device, mesh.shape["harm"], mesh.shape["tile"]),
        mesh=mesh,
        in_specs=(
            P(("design", "tile"), None, None, None, None, "harm"),
            P("design", None, None, None, "harm"),
            P("design"),
            P("design"),
        ),
        out_specs=P("design", ("harm", "tile")),
        check_vma=False,
    )
```

```python
import functools
import math

import jax
import jax.numpy as jnp
import ml_dtypes
import numpy as np
from jax import lax
from jax.experimental import pallas as pl
from jax.experimental.pallas import tpu as pltpu
from jax.sharding import PartitionSpec as P

GRID = 512
ORD = 51
HALF = 64
LANES = 128
ROWS = 24
MESH = pl.DeviceIdType.MESH


def split(value):
    high = value.astype(ml_dtypes.bfloat16)
    low = (value - high.astype(value.dtype)).astype(ml_dtypes.bfloat16)
    return high, low


def make_tables(n_harm, n_tile, depth, wide):
    harmonic = np.arange(n_harm * depth).reshape(n_harm, depth)
    order_y = harmonic // ORD - ORD // 2
    place_x = harmonic % ORD
    row_id = np.arange(n_harm * n_tile)
    angle = (order_y[:, None, :] * row_id[None, :, None] % GRID) * (2.0 * math.pi / GRID)
    twiddle = np.zeros((n_harm, n_harm * n_tile, 2, wide), np.float32)
    twiddle[:, :, 0, :depth] = np.cos(angle)
    twiddle[:, :, 1, :depth] = np.sin(angle)
    pick = np.zeros((n_harm, wide, LANES), ml_dtypes.bfloat16)
    lane = np.arange(LANES) % HALF
    pick[:, :depth, :] = place_x[:, :, None] == lane[None, None, :]
    order_x = np.arange(ORD) - ORD // 2
    angle = (order_x[:, None] * np.arange(GRID)[None, :] % GRID) * (2.0 * math.pi / GRID)
    column = np.zeros((LANES, 2 * GRID), np.float32)
    column[:ORD, :GRID] = np.cos(angle)
    column[HALF : HALF + ORD, :GRID] = -np.sin(angle)
    column[:ORD, GRID:] = np.sin(angle)
    column[HALF : HALF + ORD, GRID:] = np.cos(angle)
    return twiddle, pick, np.stack(split(column))


def kernel(
    n_harm, n_tile, fwd_ref, adj_ref, owner_ref, source_ref, twiddle_hbm, pick_hbm, column_hbm,
    out_ref, twiddle, pick, column, amp, left, send_f, send_a, recv_f, recv_a,
    load_sem, sent_f, sent_a, got_f, got_a,
):
    layers, sources, comps, _, depth = adj_ref.shape
    n_dev = n_harm * n_tile
    wide = amp.shape[-1]
    harm = lax.axis_index("harm")
    tile = lax.axis_index("tile")
    me = harm * n_tile + tile

    loads = [
        pltpu.make_async_copy(twiddle_hbm.at[harm], twiddle, load_sem.at[0]),
        pltpu.make_async_copy(pick_hbm.at[harm], pick, load_sem.at[1]),
        pltpu.make_async_copy(column_hbm, column, load_sem.at[2]),
    ]
    for load in loads:
        load.start()

    def peer(step):
        other = lax.rem(me + step, n_dev)
        return other, {"harm": other // n_tile, "tile": lax.rem(other, n_tile)}

    barrier = pltpu.get_barrier_semaphore()

    def greet(step, carry):
        pl.semaphore_signal(barrier, inc=1, device_id=peer(step)[1], device_id_type=MESH)
        return carry

    lax.fori_loop(1, n_dev, greet, 0)

    amp[...] = jnp.zeros_like(amp)
    mine = jnp.int32(0)
    for layer in range(1, layers):
        mine = jnp.where(owner_ref[layer] == tile, layer, mine)
    for source in range(sources):
        for comp in range(comps):
            row = source * comps + comp
            lines = [fwd_ref[0, mine, source_ref[source], comp]]
            lines += [adj_ref[layer, source, comp] for layer in range(layers)]
            for group, line in enumerate(lines):
                line = line.astype(jnp.float32)
                for part in range(2):
                    amp[group, part, row : row + 1, :depth] = line[part : part + 1]
    loads[0].wait()
    loads[1].wait()

    low_lanes = lax.broadcasted_iota(jnp.int32, (ROWS, LANES), 1) < HALF

    def stage(group, row_id, slot):
        cosine = twiddle[row_id, 0:1, :]
        sine = twiddle[row_id, 1:2, :]
        real, imag = amp[group, 0], amp[group, 1]
        turned = jnp.concatenate(
            [real * cosine - imag * sine, real * sine + imag * cosine], axis=0
        )
        high = turned.astype(jnp.bfloat16)
        rows = slice(slot * 2 * ROWS, (slot + 1) * 2 * ROWS)
        left[0, rows, :] = high
        left[1, rows, :] = (turned - high.astype(jnp.float32)).astype(jnp.bfloat16)

    def partial_sums(to_harm):
        for to_tile in range(n_tile):
            stage(0, to_harm * n_tile + to_tile, to_tile)
        for layer in range(layers):
            stage(1 + layer, to_harm * n_tile + tile, n_tile + layer)
        right = pick[...]
        sums = jnp.dot(left[0], right, preferred_element_type=jnp.float32) + jnp.dot(
            left[1], right, preferred_element_type=jnp.float32
        )
        packed = []
        for slot in range(n_tile + layers):
            start = slot * 2 * ROWS
            packed.append(
                jnp.where(low_lanes, sums[start : start + ROWS], sums[start + ROWS : start + 2 * ROWS])
            )
        return packed[:n_tile], packed[n_tile:]

    def copy_f(to_harm, to_tile, slot):
        return pltpu.make_async_remote_copy(
            src_ref=send_f.at[to_harm * n_tile + to_tile],
            dst_ref=recv_f.at[slot],
            send_sem=sent_f.at[to_harm * n_tile + to_tile],
            recv_sem=got_f.at[slot],
            device_id={"harm": to_harm, "tile": to_tile},
            device_id_type=MESH,
        )

    def copy_a(to_harm, slot):
        return pltpu.make_async_remote_copy(
            src_ref=send_a.at[to_harm],
            dst_ref=recv_a.at[slot],
            send_sem=sent_a.at[to_harm],
            recv_sem=got_a.at[slot],
            device_id={"harm": to_harm, "tile": tile},
            device_id_type=MESH,
        )

    def compute(to_harm):
        fwd, adj = partial_sums(to_harm)
        for to_tile in range(n_tile):
            send_f[to_harm * n_tile + to_tile] = fwd[to_tile]
        send_a[to_harm] = jnp.concatenate(adj, axis=0)

    def block(step):
        to_harm = lax.rem(harm + step, n_harm)
        compute(to_harm)
        return to_harm

    def send_block(to_harm):
        for to_tile in range(n_tile):
            copy_f(to_harm, to_tile, me).start()
        copy_a(to_harm, harm).start()

    first = block(1)
    pl.semaphore_wait(barrier, n_dev - 1)
    send_block(first)

    def away(step, carry):
        send_block(block(step))
        return carry

    lax.fori_loop(2, n_harm, away, 0)

    compute(harm)
    for step in range(1, n_tile):
        copy_f(harm, lax.rem(tile + step, n_tile), me).start()
    recv_f[me] = send_f[me]
    recv_a[harm] = send_a[harm]
    loads[2].wait()

    def arrive_f(step, carry):
        other, _ = peer(step)
        copy_f(other // n_tile, lax.rem(other, n_tile), other).wait()
        return carry

    def arrive_a(step, carry):
        other = lax.rem(harm + step, n_harm)
        copy_a(other, other).wait()
        return carry

    lax.fori_loop(1, n_dev, arrive_f, 0)
    lax.fori_loop(1, n_harm, arrive_a, 0)

    def add_f(layer):
        owner = owner_ref[layer]
        return lax.fori_loop(
            0,
            n_harm,
            lambda source, total: total + recv_f[source * n_tile + owner],
            jnp.zeros((ROWS, LANES), jnp.float32),
        )

    adj = lax.fori_loop(
        0,
        n_harm,
        lambda source, total: total + recv_a[source],
        jnp.zeros((layers * ROWS, LANES), jnp.float32),
    )
    lines = jnp.concatenate([add_f(layer) for layer in range(layers)] + [adj], axis=0)
    high = lines.astype(jnp.bfloat16)
    low = (lines - high.astype(jnp.float32)).astype(jnp.bfloat16)
    fields = (
        jnp.dot(high, column[0], preferred_element_type=jnp.float32)
        + jnp.dot(low, column[0], preferred_element_type=jnp.float32)
        + jnp.dot(high, column[1], preferred_element_type=jnp.float32)
    )
    for layer in range(layers):
        one = fields[layer * ROWS : (layer + 1) * ROWS]
        two = fields[(layers + layer) * ROWS : (layers + layer + 1) * ROWS]
        both = one * two
        out_ref[layer : layer + 1, :] = jnp.sum(
            both[:, :GRID] - both[:, GRID:], axis=0, keepdims=True
        )


def per_device(n_harm, n_tile, fwd_ckpt, adj_amp, layer_owner, source_list):
    layers, _, sources, comps, depth = adj_amp.shape
    assert sources * comps <= ROWS
    wide = -(-depth // LANES) * LANES
    n_dev = n_harm * n_tile
    twiddle, pick, column = make_tables(n_harm, n_tile, depth, wide)
    slots = n_tile + layers
    vmem = pl.BlockSpec(memory_space=pltpu.VMEM)
    smem = pl.BlockSpec(memory_space=pltpu.SMEM)
    hbm = pl.BlockSpec(memory_space=pltpu.HBM)
    fwd_ckpt = jnp.transpose(fwd_ckpt, (0, 1, 3, 4, 2, 5))
    adj_amp = jnp.transpose(adj_amp, (0, 2, 3, 1, 4))
    total = pl.pallas_call(
        functools.partial(kernel, n_harm, n_tile),
        out_shape=jax.ShapeDtypeStruct((layers, GRID), jnp.float32),
        in_specs=[vmem, vmem, smem, smem, hbm, hbm, hbm],
        out_specs=vmem,
        scratch_shapes=[
            pltpu.VMEM((n_dev, 2, wide), jnp.float32),
            pltpu.VMEM((wide, LANES), jnp.bfloat16),
            pltpu.VMEM(column.shape, jnp.bfloat16),
            pltpu.VMEM((1 + layers, 2, ROWS, wide), jnp.float32),
            pltpu.VMEM((2, slots * 2 * ROWS, wide), jnp.bfloat16),
            pltpu.VMEM((n_dev, ROWS, LANES), jnp.float32),
            pltpu.VMEM((n_harm, layers * ROWS, LANES), jnp.float32),
            pltpu.VMEM((n_dev, ROWS, LANES), jnp.float32),
            pltpu.VMEM((n_harm, layers * ROWS, LANES), jnp.float32),
            pltpu.SemaphoreType.DMA((3,)),
            pltpu.SemaphoreType.DMA((n_dev,)),
            pltpu.SemaphoreType.DMA((n_harm,)),
            pltpu.SemaphoreType.DMA((n_dev,)),
            pltpu.SemaphoreType.DMA((n_harm,)),
        ],
        compiler_params=pltpu.CompilerParams(
            collective_id=0, has_side_effects=True, vmem_limit_bytes=63 * 1024 * 1024
        ),
    )(
        fwd_ckpt, adj_amp, layer_owner, source_list,
        jnp.asarray(twiddle), jnp.asarray(pick), jnp.asarray(column),
    )
    return total * jnp.float32((sources * comps) ** (-0.5))


def solution(mesh):
    return jax.shard_map(
        functools.partial(per_device, mesh.shape["harm"], mesh.shape["tile"]),
        mesh=mesh,
        in_specs=(
            P(("design", "tile"), None, None, None, None, "harm"),
            P("design", None, None, None, "harm"),
            P("design"),
            P("design"),
        ),
        out_specs=P("design", ("harm", "tile")),
        check_vma=False,
    )
```

```python
import functools
import math

import jax
import jax.numpy as jnp
import ml_dtypes
import numpy as np
from jax import lax
from jax.experimental import pallas as pl
from jax.experimental.pallas import tpu as pltpu
from jax.sharding import PartitionSpec as P

GRID = 512
ORD = 51
HALF = 64
LANES = 128
ROWS = 24
MESH = pl.DeviceIdType.MESH


def split(value):
    high = value.astype(ml_dtypes.bfloat16)
    low = (value - high.astype(value.dtype)).astype(ml_dtypes.bfloat16)
    return high, low


def make_tables(n_harm, n_tile, depth, wide):
    harmonic = np.arange(n_harm * depth).reshape(n_harm, depth)
    order_y = harmonic // ORD - ORD // 2
    place_x = harmonic % ORD
    row_id = np.arange(n_harm * n_tile)
    angle = (order_y[:, None, :] * row_id[None, :, None] % GRID) * (2.0 * math.pi / GRID)
    twiddle = np.zeros((n_harm, n_harm * n_tile, 2, wide), np.float32)
    twiddle[:, :, 0, :depth] = np.cos(angle)
    twiddle[:, :, 1, :depth] = np.sin(angle)
    pick = np.zeros((n_harm, wide, LANES), ml_dtypes.bfloat16)
    lane = np.arange(LANES) % HALF
    pick[:, :depth, :] = place_x[:, :, None] == lane[None, None, :]
    order_x = np.arange(ORD) - ORD // 2
    angle = (order_x[:, None] * np.arange(GRID)[None, :] % GRID) * (2.0 * math.pi / GRID)
    column = np.zeros((LANES, 2 * GRID), np.float32)
    column[:ORD, :GRID] = np.cos(angle)
    column[HALF : HALF + ORD, :GRID] = -np.sin(angle)
    column[:ORD, GRID:] = np.sin(angle)
    column[HALF : HALF + ORD, GRID:] = np.cos(angle)
    return twiddle, pick, np.stack(split(column))


def loop(first, end, body):
    if end - first <= 16:
        for step in range(first, end):
            body(step)
    else:
        lax.fori_loop(first, end, lambda step, carry: (body(step), carry)[1], 0)


def kernel(
    n_harm, n_tile, fwd_hbm, adj_hbm, owner_hbm, source_hbm, twiddle_hbm, pick_hbm, column_hbm,
    out_ref, fwd_ref, adj_ref, owner_ref, source_ref, twiddle, pick, column, amp, left, send_f, send_a, recv_f, recv_a,
    load_sem, sent_f, sent_a, got_f, got_a,
):
    layers, sources, comps, _, depth = adj_ref.shape
    n_dev = n_harm * n_tile
    wide = amp.shape[-1]
    harm = lax.axis_index("harm")
    tile = lax.axis_index("tile")
    me = harm * n_tile + tile

    def peer(step):
        other = lax.rem(me + step, n_dev)
        return other, {"harm": other // n_tile, "tile": lax.rem(other, n_tile)}

    barrier = pltpu.get_barrier_semaphore()

    def greet(step):
        pl.semaphore_signal(barrier, inc=1, device_id=peer(step)[1], device_id_type=MESH)

    loop(1, n_dev, greet)

    loads = [
        pltpu.make_async_copy(source, target, load_sem.at[index])
        for index, (source, target) in enumerate(
            [
                (owner_hbm, owner_ref),
                (source_hbm, source_ref),
                (fwd_hbm, fwd_ref),
                (adj_hbm, adj_ref),
                (twiddle_hbm.at[harm], twiddle),
                (pick_hbm.at[harm], pick),
                (column_hbm, column),
            ]
        )
    ]
    for load in loads:
        load.start()

    amp[...] = jnp.zeros_like(amp)
    for load in loads[:4]:
        load.wait()
    mine = jnp.int32(0)
    for layer in range(1, layers):
        mine = jnp.where(owner_ref[layer] == tile, layer, mine)
    for source in range(sources):
        for comp in range(comps):
            row = source * comps + comp
            lines = [fwd_ref[0, mine, source_ref[source], comp]]
            lines += [adj_ref[layer, source, comp] for layer in range(layers)]
            for group, line in enumerate(lines):
                line = line.astype(jnp.float32)
                for part in range(2):
                    amp[group, part, row : row + 1, :depth] = line[part : part + 1]
    loads[4].wait()
    loads[5].wait()

    low_lanes = lax.broadcasted_iota(jnp.int32, (ROWS, LANES), 1) < HALF

    def stage(group, row_id, slot):
        cosine = twiddle[row_id, 0:1, :]
        sine = twiddle[row_id, 1:2, :]
        real, imag = amp[group, 0], amp[group, 1]
        turned = jnp.concatenate(
            [real * cosine - imag * sine, real * sine + imag * cosine], axis=0
        )
        high = turned.astype(jnp.bfloat16)
        rows = slice(slot * 2 * ROWS, (slot + 1) * 2 * ROWS)
        left[0, rows, :] = high
        left[1, rows, :] = (turned - high.astype(jnp.float32)).astype(jnp.bfloat16)

    def partial_sums(to_harm):
        for to_tile in range(n_tile):
            stage(0, to_harm * n_tile + to_tile, to_tile)
        for layer in range(layers):
            stage(1 + layer, to_harm * n_tile + tile, n_tile + layer)
        right = pick[...]
        sums = jnp.dot(left[0], right, preferred_element_type=jnp.float32) + jnp.dot(
            left[1], right, preferred_element_type=jnp.float32
        )
        packed = []
        for slot in range(n_tile + layers):
            start = slot * 2 * ROWS
            packed.append(
                jnp.where(low_lanes, sums[start : start + ROWS], sums[start + ROWS : start + 2 * ROWS])
            )
        return packed[:n_tile], packed[n_tile:]

    def copy_f(to_harm, to_tile, slot):
        return pltpu.make_async_remote_copy(
            src_ref=send_f.at[to_harm * n_tile + to_tile],
            dst_ref=recv_f.at[slot],
            send_sem=sent_f.at[to_harm * n_tile + to_tile],
            recv_sem=got_f.at[slot],
            device_id={"harm": to_harm, "tile": to_tile},
            device_id_type=MESH,
        )

    def copy_a(to_harm, slot):
        return pltpu.make_async_remote_copy(
            src_ref=send_a.at[to_harm],
            dst_ref=recv_a.at[slot],
            send_sem=sent_a.at[to_harm],
            recv_sem=got_a.at[slot],
            device_id={"harm": to_harm, "tile": tile},
            device_id_type=MESH,
        )

    def compute(to_harm):
        fwd, adj = partial_sums(to_harm)
        for to_tile in range(n_tile):
            send_f[to_harm * n_tile + to_tile] = fwd[to_tile].astype(jnp.bfloat16)
        send_a[to_harm] = jnp.concatenate(adj, axis=0).astype(jnp.bfloat16)

    def block(step):
        to_harm = lax.rem(harm + step, n_harm)
        compute(to_harm)
        return to_harm

    def send_block(to_harm):
        for to_tile in range(n_tile):
            copy_f(to_harm, to_tile, me).start()
        copy_a(to_harm, harm).start()

    first = block(1)
    pl.semaphore_wait(barrier, n_dev - 1)
    send_block(first)

    loop(2, n_harm, lambda step: send_block(block(step)))

    compute(harm)
    for step in range(1, n_tile):
        copy_f(harm, lax.rem(tile + step, n_tile), me).start()
    recv_f[me] = send_f[me]
    recv_a[harm] = send_a[harm]
    loads[6].wait()

    def arrive_f(step):
        other, _ = peer(step)
        copy_f(other // n_tile, lax.rem(other, n_tile), other).wait()

    def arrive_a(step):
        other = lax.rem(harm + step, n_harm)
        copy_a(other, other).wait()

    loop(1, n_dev, arrive_f)
    loop(1, n_harm, arrive_a)

    def add_f(layer):
        owner = owner_ref[layer]
        return lax.fori_loop(
            0,
            n_harm,
            lambda source, total: total + recv_f[source * n_tile + owner].astype(jnp.float32),
            jnp.zeros((ROWS, LANES), jnp.float32),
        )

    adj = lax.fori_loop(
        0,
        n_harm,
        lambda source, total: total + recv_a[source].astype(jnp.float32),
        jnp.zeros((layers * ROWS, LANES), jnp.float32),
    )
    lines = jnp.concatenate([add_f(layer) for layer in range(layers)] + [adj], axis=0)
    high = lines.astype(jnp.bfloat16)
    low = (lines - high.astype(jnp.float32)).astype(jnp.bfloat16)
    fields = (
        jnp.dot(high, column[0], preferred_element_type=jnp.float32)
        + jnp.dot(low, column[0], preferred_element_type=jnp.float32)
        + jnp.dot(high, column[1], preferred_element_type=jnp.float32)
    )
    for layer in range(layers):
        one = fields[layer * ROWS : (layer + 1) * ROWS]
        two = fields[(layers + layer) * ROWS : (layers + layer + 1) * ROWS]
        both = one * two
        out_ref[layer : layer + 1, :] = jnp.sum(
            both[:, :GRID] - both[:, GRID:], axis=0, keepdims=True
        )


def per_device(n_harm, n_tile, fwd_ckpt, adj_amp, layer_owner, source_list):
    layers, _, sources, comps, depth = adj_amp.shape
    assert sources * comps <= ROWS
    wide = -(-depth // LANES) * LANES
    n_dev = n_harm * n_tile
    twiddle, pick, column = make_tables(n_harm, n_tile, depth, wide)
    slots = n_tile + layers
    vmem = pl.BlockSpec(memory_space=pltpu.VMEM)
    hbm = pl.BlockSpec(memory_space=pltpu.HBM)
    fwd_ckpt = jnp.transpose(fwd_ckpt, (0, 1, 3, 4, 2, 5))
    adj_amp = jnp.transpose(adj_amp, (0, 2, 3, 1, 4))
    total = pl.pallas_call(
        functools.partial(kernel, n_harm, n_tile),
        out_shape=jax.ShapeDtypeStruct((layers, GRID), jnp.float32),
        in_specs=[hbm] * 7,
        out_specs=vmem,
        scratch_shapes=[
            pltpu.VMEM(fwd_ckpt.shape, jnp.bfloat16),
            pltpu.VMEM(adj_amp.shape, jnp.bfloat16),
            pltpu.SMEM(layer_owner.shape, jnp.int32),
            pltpu.SMEM(source_list.shape, jnp.int32),
            pltpu.VMEM((n_dev, 2, wide), jnp.float32),
            pltpu.VMEM((wide, LANES), jnp.bfloat16),
            pltpu.VMEM(column.shape, jnp.bfloat16),
            pltpu.VMEM((1 + layers, 2, ROWS, wide), jnp.float32),
            pltpu.VMEM((2, slots * 2 * ROWS, wide), jnp.bfloat16),
            pltpu.VMEM((n_dev, ROWS, LANES), jnp.bfloat16),
            pltpu.VMEM((n_harm, layers * ROWS, LANES), jnp.bfloat16),
            pltpu.VMEM((n_dev, ROWS, LANES), jnp.bfloat16),
            pltpu.VMEM((n_harm, layers * ROWS, LANES), jnp.bfloat16),
            pltpu.SemaphoreType.DMA((7,)),
            pltpu.SemaphoreType.DMA((n_dev,)),
            pltpu.SemaphoreType.DMA((n_harm,)),
            pltpu.SemaphoreType.DMA((n_dev,)),
            pltpu.SemaphoreType.DMA((n_harm,)),
        ],
        compiler_params=pltpu.CompilerParams(
            collective_id=0, has_side_effects=True, vmem_limit_bytes=63 * 1024 * 1024
        ),
    )(
        fwd_ckpt, adj_amp, layer_owner, source_list,
        jnp.asarray(twiddle), jnp.asarray(pick), jnp.asarray(column),
    )
    return total * jnp.float32((sources * comps) ** (-0.5))


def solution(mesh):
    return jax.shard_map(
        functools.partial(per_device, mesh.shape["harm"], mesh.shape["tile"]),
        mesh=mesh,
        in_specs=(
            P(("design", "tile"), None, None, None, None, "harm"),
            P("design", None, None, None, "harm"),
            P("design"),
            P("design"),
        ),
        out_specs=P("design", ("harm", "tile")),
        check_vma=False,
    )
```

```python
import functools
import math

import jax
import jax.numpy as jnp
import ml_dtypes
import numpy as np
from jax import lax
from jax.experimental import pallas as pl
from jax.experimental.pallas import tpu as pltpu
from jax.sharding import PartitionSpec as P

GRID = 512
ORD = 51
HALF = 64
LANES = 128
ROWS = 24
MESH = pl.DeviceIdType.MESH


def split(value):
    high = value.astype(ml_dtypes.bfloat16)
    low = (value - high.astype(value.dtype)).astype(ml_dtypes.bfloat16)
    return high, low


def make_tables(n_harm, n_tile, depth, wide):
    harmonic = np.arange(n_harm * depth).reshape(n_harm, depth)
    order_y = harmonic // ORD - ORD // 2
    place_x = harmonic % ORD
    row_id = np.arange(n_harm * n_tile)
    angle = (order_y[:, None, :] * row_id[None, :, None] % GRID) * (2.0 * math.pi / GRID)
    twiddle = np.zeros((n_harm, n_harm * n_tile, 2, wide), np.float32)
    twiddle[:, :, 0, :depth] = np.cos(angle)
    twiddle[:, :, 1, :depth] = np.sin(angle)
    pick = np.zeros((n_harm, wide, LANES), ml_dtypes.bfloat16)
    lane = np.arange(LANES) % HALF
    pick[:, :depth, :] = place_x[:, :, None] == lane[None, None, :]
    order_x = np.arange(ORD) - ORD // 2
    angle = (order_x[:, None] * np.arange(GRID)[None, :] % GRID) * (2.0 * math.pi / GRID)
    column = np.zeros((LANES, 2 * GRID), np.float32)
    column[:ORD, :GRID] = np.cos(angle)
    column[HALF : HALF + ORD, :GRID] = -np.sin(angle)
    column[:ORD, GRID:] = np.sin(angle)
    column[HALF : HALF + ORD, GRID:] = np.cos(angle)
    return twiddle, pick, np.stack(split(column))


def loop(first, end, body):
    if end - first <= 16:
        for step in range(first, end):
            body(step)
    else:
        lax.fori_loop(first, end, lambda step, carry: (body(step), carry)[1], 0)


def kernel(
    n_harm, n_tile, fwd_hbm, adj_hbm, owner_hbm, source_hbm, twiddle_hbm, pick_hbm, column_hbm,
    out_ref, fwd_ref, adj_ref, owner_ref, source_ref, twiddle, pick, column, amp, left, send_f, send_a, recv_f, recv_a,
    load_sem, sent_f, sent_a, got_f, got_a,
):
    layers, sources, comps, _, depth = adj_ref.shape
    n_dev = n_harm * n_tile
    wide = amp.shape[-1]
    harm = lax.axis_index("harm")
    tile = lax.axis_index("tile")
    me = harm * n_tile + tile

    def peer(step):
        other = lax.rem(me + step, n_dev)
        return other, {"harm": other // n_tile, "tile": lax.rem(other, n_tile)}

    barrier = pltpu.get_barrier_semaphore()

    def greet(step):
        pl.semaphore_signal(barrier, inc=1, device_id=peer(step)[1], device_id_type=MESH)

    loop(1, n_dev, greet)

    loads = [
        pltpu.make_async_copy(source, target, load_sem.at[index])
        for index, (source, target) in enumerate(
            [
                (owner_hbm, owner_ref),
                (source_hbm, source_ref),
                (fwd_hbm, fwd_ref),
                (adj_hbm, adj_ref),
                (twiddle_hbm.at[harm], twiddle),
                (pick_hbm.at[harm], pick),
                (column_hbm, column),
            ]
        )
    ]
    for load in loads:
        load.start()

    amp[...] = jnp.zeros_like(amp)
    for load in loads[:4]:
        load.wait()
    mine = jnp.int32(0)
    for layer in range(1, layers):
        mine = jnp.where(owner_ref[layer] == tile, layer, mine)
    for source in range(sources):
        for comp in range(comps):
            row = source * comps + comp
            lines = [fwd_ref[0, mine, source_ref[source], comp]]
            lines += [adj_ref[layer, source, comp] for layer in range(layers)]
            for group, line in enumerate(lines):
                line = line.astype(jnp.float32)
                for part in range(2):
                    amp[group, part, row : row + 1, :depth] = line[part : part + 1]
    loads[4].wait()
    loads[5].wait()

    low_lanes = lax.broadcasted_iota(jnp.int32, (ROWS, LANES), 1) < HALF

    def stage(group, row_id, slot):
        cosine = twiddle[row_id, 0:1, :]
        sine = twiddle[row_id, 1:2, :]
        real, imag = amp[group, 0], amp[group, 1]
        turned = jnp.concatenate(
            [real * cosine - imag * sine, real * sine + imag * cosine], axis=0
        )
        high = turned.astype(jnp.bfloat16)
        rows = slice(slot * 2 * ROWS, (slot + 1) * 2 * ROWS)
        left[0, rows, :] = high
        left[1, rows, :] = (turned - high.astype(jnp.float32)).astype(jnp.bfloat16)

    def partial_sums(to_harm):
        for to_tile in range(n_tile):
            stage(0, to_harm * n_tile + to_tile, to_tile)
        for layer in range(layers):
            stage(1 + layer, to_harm * n_tile + tile, n_tile + layer)
        right = pick[...]
        sums = jnp.dot(left[0], right, preferred_element_type=jnp.float32) + jnp.dot(
            left[1], right, preferred_element_type=jnp.float32
        )
        packed = []
        for slot in range(n_tile + layers):
            start = slot * 2 * ROWS
            packed.append(
                jnp.where(low_lanes, sums[start : start + ROWS], sums[start + ROWS : start + 2 * ROWS])
            )
        return packed[:n_tile], packed[n_tile:]

    def copy_f(to_harm, to_tile, slot):
        return pltpu.make_async_remote_copy(
            src_ref=send_f.at[to_harm * n_tile + to_tile],
            dst_ref=recv_f.at[slot],
            send_sem=sent_f.at[to_harm * n_tile + to_tile],
            recv_sem=got_f.at[slot],
            device_id={"harm": to_harm, "tile": to_tile},
            device_id_type=MESH,
        )

    def copy_a(to_harm, slot):
        return pltpu.make_async_remote_copy(
            src_ref=send_a.at[to_harm],
            dst_ref=recv_a.at[slot],
            send_sem=sent_a.at[to_harm],
            recv_sem=got_a.at[slot],
            device_id={"harm": to_harm, "tile": tile},
            device_id_type=MESH,
        )

    def compute(to_harm):
        fwd, adj = partial_sums(to_harm)
        for to_tile in range(n_tile):
            send_f[to_harm * n_tile + to_tile] = fwd[to_tile].astype(jnp.bfloat16)
        send_a[to_harm] = jnp.concatenate(adj, axis=0).astype(jnp.bfloat16)

    def block(step):
        to_harm = lax.rem(harm + step, n_harm)
        compute(to_harm)
        return to_harm

    def send_block(to_harm):
        for to_tile in range(n_tile):
            copy_f(to_harm, to_tile, me).start()
        copy_a(to_harm, harm).start()

    first = block(1)
    pl.semaphore_wait(barrier, n_dev - 1)
    send_block(first)

    loop(2, n_harm, lambda step: send_block(block(step)))

    compute(harm)
    for step in range(1, n_tile):
        copy_f(harm, lax.rem(tile + step, n_tile), me).start()
    recv_f[me] = send_f[me]
    recv_a[harm] = send_a[harm]
    loads[6].wait()

    def arrive_f(step):
        other, _ = peer(step)
        copy_f(other // n_tile, lax.rem(other, n_tile), other).wait()

    def arrive_a(step):
        other = lax.rem(harm + step, n_harm)
        copy_a(other, other).wait()

    loop(1, n_dev, arrive_f)
    loop(1, n_harm, arrive_a)

    def add_f(layer):
        owner = owner_ref[layer]
        return lax.fori_loop(
            0,
            n_harm,
            lambda source, total: total + recv_f[source * n_tile + owner].astype(jnp.float32),
            jnp.zeros((ROWS, LANES), jnp.float32),
        )

    adj = lax.fori_loop(
        0,
        n_harm,
        lambda source, total: total + recv_a[source].astype(jnp.float32),
        jnp.zeros((layers * ROWS, LANES), jnp.float32),
    )
    lines = jnp.concatenate([add_f(layer) for layer in range(layers)] + [adj], axis=0)
    high = lines.astype(jnp.bfloat16)
    low = (lines - high.astype(jnp.float32)).astype(jnp.bfloat16)
    fields = (
        jnp.dot(high, column[0], preferred_element_type=jnp.float32)
        + jnp.dot(low, column[0], preferred_element_type=jnp.float32)
        + jnp.dot(high, column[1], preferred_element_type=jnp.float32)
    )
    for layer in range(layers):
        one = fields[layer * ROWS : (layer + 1) * ROWS]
        two = fields[(layers + layer) * ROWS : (layers + layer + 1) * ROWS]
        both = one * two
        out_ref[layer : layer + 1, :] = jnp.sum(
            both[:, :GRID] - both[:, GRID:], axis=0, keepdims=True
        )


def per_device(n_harm, n_tile, fwd_ckpt, adj_amp, layer_owner, source_list):
    layers, _, sources, comps, depth = adj_amp.shape
    assert sources * comps <= ROWS
    wide = -(-depth // LANES) * LANES
    n_dev = n_harm * n_tile
    twiddle, pick, column = make_tables(n_harm, n_tile, depth, wide)
    slots = n_tile + layers
    vmem = pl.BlockSpec(memory_space=pltpu.VMEM)
    hbm = pl.BlockSpec(memory_space=pltpu.HBM)
    fwd_ckpt = jnp.transpose(fwd_ckpt, (0, 1, 3, 4, 2, 5))
    adj_amp = jnp.transpose(adj_amp, (0, 2, 3, 1, 4))
    total = pl.pallas_call(
        functools.partial(kernel, n_harm, n_tile),
        out_shape=jax.ShapeDtypeStruct((layers, GRID), jnp.float32),
        in_specs=[hbm] * 7,
        out_specs=vmem,
        scratch_shapes=[
            pltpu.VMEM(fwd_ckpt.shape, jnp.bfloat16),
            pltpu.VMEM(adj_amp.shape, jnp.bfloat16),
            pltpu.SMEM(layer_owner.shape, jnp.int32),
            pltpu.SMEM(source_list.shape, jnp.int32),
            pltpu.VMEM((n_dev, 2, wide), jnp.float32),
            pltpu.VMEM((wide, LANES), jnp.bfloat16),
            pltpu.VMEM(column.shape, jnp.bfloat16),
            pltpu.VMEM((1 + layers, 2, ROWS, wide), jnp.float32),
            pltpu.VMEM((2, slots * 2 * ROWS, wide), jnp.bfloat16),
            pltpu.VMEM((n_dev, ROWS, LANES), jnp.bfloat16),
            pltpu.VMEM((n_harm, layers * ROWS, LANES), jnp.bfloat16),
            pltpu.VMEM((n_dev, ROWS, LANES), jnp.bfloat16),
            pltpu.VMEM((n_harm, layers * ROWS, LANES), jnp.bfloat16),
            pltpu.SemaphoreType.DMA((7,)),
            pltpu.SemaphoreType.DMA((n_dev,)),
            pltpu.SemaphoreType.DMA((n_harm,)),
            pltpu.SemaphoreType.DMA((n_dev,)),
            pltpu.SemaphoreType.DMA((n_harm,)),
        ],
        compiler_params=pltpu.CompilerParams(
            collective_id=0, has_side_effects=True, vmem_limit_bytes=24 * 1024 * 1024
        ),
    )(
        *[
            pltpu.with_memory_space_constraint(value, pltpu.HBM)
            for value in (
                fwd_ckpt, adj_amp, layer_owner, source_list,
                jnp.asarray(twiddle), jnp.asarray(pick), jnp.asarray(column),
            )
        ]
    )
    return total * jnp.float32((sources * comps) ** (-0.5))


def solution(mesh):
    return jax.shard_map(
        functools.partial(per_device, mesh.shape["harm"], mesh.shape["tile"]),
        mesh=mesh,
        in_specs=(
            P(("design", "tile"), None, None, None, None, "harm"),
            P("design", None, None, None, "harm"),
            P("design"),
            P("design"),
        ),
        out_specs=P("design", ("harm", "tile")),
        check_vma=False,
    )
```

```python
import functools
import math

import jax
import jax.numpy as jnp
import ml_dtypes
import numpy as np
from jax import lax
from jax.experimental import pallas as pl
from jax.experimental.pallas import tpu as pltpu
from jax.sharding import PartitionSpec as P

GRID = 512
ORD = 51
HALF = 64
LANES = 128
ROWS = 24
MESH = pl.DeviceIdType.MESH


def split(value):
    high = value.astype(ml_dtypes.bfloat16)
    low = (value - high.astype(value.dtype)).astype(ml_dtypes.bfloat16)
    return high, low


def make_tables(n_harm, n_tile, depth, wide):
    harmonic = np.arange(n_harm * depth).reshape(n_harm, depth)
    order_y = harmonic // ORD - ORD // 2
    place_x = harmonic % ORD
    row_id = np.arange(n_harm * n_tile)
    angle = (order_y[:, None, :] * row_id[None, :, None] % GRID) * (2.0 * math.pi / GRID)
    twiddle = np.zeros((n_harm, n_harm * n_tile, 2, wide), np.float32)
    twiddle[:, :, 0, :depth] = np.cos(angle)
    twiddle[:, :, 1, :depth] = np.sin(angle)
    pick = np.zeros((n_harm, wide, LANES), ml_dtypes.bfloat16)
    lane = np.arange(LANES) % HALF
    pick[:, :depth, :] = place_x[:, :, None] == lane[None, None, :]
    order_x = np.arange(ORD) - ORD // 2
    angle = (order_x[:, None] * np.arange(GRID)[None, :] % GRID) * (2.0 * math.pi / GRID)
    column = np.zeros((LANES, 2 * GRID), np.float32)
    column[:ORD, :GRID] = np.cos(angle)
    column[HALF : HALF + ORD, :GRID] = -np.sin(angle)
    column[:ORD, GRID:] = np.sin(angle)
    column[HALF : HALF + ORD, GRID:] = np.cos(angle)
    return twiddle, pick, np.stack(split(column))


def loop(first, end, body):
    if end - first <= 16:
        for step in range(first, end):
            body(step)
    else:
        lax.fori_loop(first, end, lambda step, carry: (body(step), carry)[1], 0)


def kernel(
    n_harm, n_tile, fwd_hbm, adj_hbm, owner_hbm, source_hbm, twiddle_hbm, pick_hbm, column_hbm,
    out_ref, fwd_ref, adj_ref, owner_ref, source_ref, twiddle, pick, column, amp, left, send_f, send_a, recv_f, recv_a,
    load_sem, sent_f, sent_a, got_f, got_a,
):
    layers, sources, comps, _, depth = adj_ref.shape
    n_dev = n_harm * n_tile
    wide = amp.shape[-1]
    harm = lax.axis_index("harm")
    tile = lax.axis_index("tile")
    me = harm * n_tile + tile

    def peer(step):
        other = lax.rem(me + step, n_dev)
        return other, {"harm": other // n_tile, "tile": lax.rem(other, n_tile)}

    barrier = pltpu.get_barrier_semaphore()

    def greet(step):
        pl.semaphore_signal(barrier, inc=1, device_id=peer(step)[1], device_id_type=MESH)

    loop(1, n_dev, greet)

    loads = [
        pltpu.make_async_copy(source, target, load_sem.at[index])
        for index, (source, target) in enumerate(
            [
                (owner_hbm, owner_ref),
                (source_hbm, source_ref),
                (fwd_hbm, fwd_ref),
                (adj_hbm, adj_ref),
                (twiddle_hbm.at[harm], twiddle),
                (pick_hbm.at[harm], pick),
                (column_hbm, column),
            ]
        )
    ]
    for load in loads:
        load.start()

    amp[...] = jnp.zeros_like(amp)
    for load in loads[:4]:
        load.wait()
    mine = jnp.int32(0)
    for layer in range(1, layers):
        mine = jnp.where(owner_ref[layer] == tile, layer, mine)
    for source in range(sources):
        for comp in range(comps):
            row = source * comps + comp
            lines = [fwd_ref[0, mine, source_ref[source], comp]]
            lines += [adj_ref[layer, source, comp] for layer in range(layers)]
            for group, line in enumerate(lines):
                line = line.astype(jnp.float32)
                for part in range(2):
                    amp[group, part, row : row + 1, :depth] = line[part : part + 1]
    loads[4].wait()
    loads[5].wait()

    low_lanes = lax.broadcasted_iota(jnp.int32, (ROWS, LANES), 1) < HALF

    def stage(group, row_id, slot):
        cosine = twiddle[row_id, 0:1, :]
        sine = twiddle[row_id, 1:2, :]
        real, imag = amp[group, 0], amp[group, 1]
        turned = jnp.concatenate(
            [real * cosine - imag * sine, real * sine + imag * cosine], axis=0
        )
        high = turned.astype(jnp.bfloat16)
        rows = slice(slot * 2 * ROWS, (slot + 1) * 2 * ROWS)
        left[0, rows, :] = high
        left[1, rows, :] = (turned - high.astype(jnp.float32)).astype(jnp.bfloat16)

    def partial_sums(to_harm):
        for to_tile in range(n_tile):
            stage(0, to_harm * n_tile + to_tile, to_tile)
        for layer in range(layers):
            stage(1 + layer, to_harm * n_tile + tile, n_tile + layer)
        right = pick[...]
        sums = jnp.dot(left[0], right, preferred_element_type=jnp.float32) + jnp.dot(
            left[1], right, preferred_element_type=jnp.float32
        )
        packed = []
        for slot in range(n_tile + layers):
            start = slot * 2 * ROWS
            packed.append(
                jnp.where(low_lanes, sums[start : start + ROWS], sums[start + ROWS : start + 2 * ROWS])
            )
        return packed[:n_tile], packed[n_tile:]

    def copy_f(to_harm, to_tile, slot):
        return pltpu.make_async_remote_copy(
            src_ref=send_f.at[to_harm * n_tile + to_tile],
            dst_ref=recv_f.at[slot],
            send_sem=sent_f.at[to_harm * n_tile + to_tile],
            recv_sem=got_f.at[slot],
            device_id={"harm": to_harm, "tile": to_tile},
            device_id_type=MESH,
        )

    def copy_a(to_harm, slot):
        return pltpu.make_async_remote_copy(
            src_ref=send_a.at[to_harm],
            dst_ref=recv_a.at[slot],
            send_sem=sent_a.at[to_harm],
            recv_sem=got_a.at[slot],
            device_id={"harm": to_harm, "tile": tile},
            device_id_type=MESH,
        )

    def compute(to_harm):
        fwd, adj = partial_sums(to_harm)
        for to_tile in range(n_tile):
            send_f[to_harm * n_tile + to_tile] = fwd[to_tile].astype(jnp.bfloat16)
        lines = [one[: sources * comps] for one in adj]
        spare = send_a.shape[1] - layers * sources * comps
        if spare:
            lines.append(jnp.zeros((spare, LANES), jnp.float32))
        send_a[to_harm] = jnp.concatenate(lines, axis=0).astype(jnp.bfloat16)

    def block(step):
        to_harm = lax.rem(harm + step, n_harm)
        compute(to_harm)
        return to_harm

    def send_block(to_harm):
        copy_a(to_harm, harm).start()
        for to_tile in range(n_tile):
            copy_f(to_harm, to_tile, me).start()

    first = block(1)
    pl.semaphore_wait(barrier, n_dev - 1)
    send_block(first)

    loop(2, n_harm, lambda step: send_block(block(step)))

    compute(harm)
    for step in range(1, n_tile):
        copy_f(harm, lax.rem(tile + step, n_tile), me).start()
    recv_f[me] = send_f[me]
    recv_a[harm] = send_a[harm]
    loads[6].wait()

    def arrive_f(step):
        other, _ = peer(step)
        copy_f(other // n_tile, lax.rem(other, n_tile), other).wait()

    def arrive_a(step):
        other = lax.rem(harm + step, n_harm)
        copy_a(other, other).wait()

    loop(1, n_dev, arrive_f)
    loop(1, n_harm, arrive_a)

    def add(part, shape):
        if n_harm <= 16:
            return sum(part(source).astype(jnp.float32) for source in range(n_harm))
        return lax.fori_loop(
            0,
            n_harm,
            lambda source, total: total + part(source).astype(jnp.float32),
            jnp.zeros(shape, jnp.float32),
        )

    def add_f(layer):
        owner = owner_ref[layer]
        return add(lambda source: recv_f[source * n_tile + owner], (ROWS, LANES))

    adj = add(lambda source: recv_a[source], recv_a.shape[1:])
    lines = jnp.concatenate([add_f(layer) for layer in range(layers)] + [adj], axis=0)
    high = lines.astype(jnp.bfloat16)
    low = (lines - high.astype(jnp.float32)).astype(jnp.bfloat16)
    fields = (
        jnp.dot(high, column[0], preferred_element_type=jnp.float32)
        + jnp.dot(low, column[0], preferred_element_type=jnp.float32)
        + jnp.dot(high, column[1], preferred_element_type=jnp.float32)
    )
    for layer in range(layers):
        rows = sources * comps
        one = fields[layer * ROWS : layer * ROWS + rows]
        two = fields[layers * ROWS + layer * rows : layers * ROWS + (layer + 1) * rows]
        both = one * two
        out_ref[layer : layer + 1, :] = jnp.sum(
            both[:, :GRID] - both[:, GRID:], axis=0, keepdims=True
        )


def per_device(n_harm, n_tile, fwd_ckpt, adj_amp, layer_owner, source_list):
    layers, _, sources, comps, depth = adj_amp.shape
    assert sources * comps <= ROWS
    wide = -(-depth // LANES) * LANES
    n_dev = n_harm * n_tile
    twiddle, pick, column = make_tables(n_harm, n_tile, depth, wide)
    slots = n_tile + layers
    vmem = pl.BlockSpec(memory_space=pltpu.VMEM)
    hbm = pl.BlockSpec(memory_space=pltpu.HBM)
    fwd_ckpt = jnp.transpose(fwd_ckpt, (0, 1, 3, 4, 2, 5))
    adj_amp = jnp.transpose(adj_amp, (0, 2, 3, 1, 4))
    total = pl.pallas_call(
        functools.partial(kernel, n_harm, n_tile),
        out_shape=jax.ShapeDtypeStruct((layers, GRID), jnp.float32),
        in_specs=[hbm] * 7,
        out_specs=vmem,
        scratch_shapes=[
            pltpu.VMEM(fwd_ckpt.shape, jnp.bfloat16),
            pltpu.VMEM(adj_amp.shape, jnp.bfloat16),
            pltpu.SMEM(layer_owner.shape, jnp.int32),
            pltpu.SMEM(source_list.shape, jnp.int32),
            pltpu.VMEM((n_dev, 2, wide), jnp.float32),
            pltpu.VMEM((wide, LANES), jnp.bfloat16),
            pltpu.VMEM(column.shape, jnp.bfloat16),
            pltpu.VMEM((1 + layers, 2, ROWS, wide), jnp.float32),
            pltpu.VMEM((2, slots * 2 * ROWS, wide), jnp.bfloat16),
            pltpu.VMEM((n_dev, ROWS, LANES), jnp.bfloat16),
            pltpu.VMEM((n_harm, -(-layers * sources * comps // 8) * 8, LANES), jnp.bfloat16),
            pltpu.VMEM((n_dev, ROWS, LANES), jnp.bfloat16),
            pltpu.VMEM((n_harm, -(-layers * sources * comps // 8) * 8, LANES), jnp.bfloat16),
            pltpu.SemaphoreType.DMA((7,)),
            pltpu.SemaphoreType.DMA((n_dev,)),
            pltpu.SemaphoreType.DMA((n_harm,)),
            pltpu.SemaphoreType.DMA((n_dev,)),
            pltpu.SemaphoreType.DMA((n_harm,)),
        ],
        compiler_params=pltpu.CompilerParams(
            collective_id=0, has_side_effects=True, vmem_limit_bytes=24 * 1024 * 1024
        ),
    )(
        *[
            pltpu.with_memory_space_constraint(value, pltpu.HBM)
            for value in (
                fwd_ckpt, adj_amp, layer_owner, source_list,
                jnp.asarray(twiddle), jnp.asarray(pick), jnp.asarray(column),
            )
        ]
    )
    return total * jnp.float32((sources * comps) ** (-0.5))


def solution(mesh):
    return jax.shard_map(
        functools.partial(per_device, mesh.shape["harm"], mesh.shape["tile"]),
        mesh=mesh,
        in_specs=(
            P(("design", "tile"), None, None, None, None, "harm"),
            P("design", None, None, None, "harm"),
            P("design"),
            P("design"),
        ),
        out_specs=P("design", ("harm", "tile")),
        check_vma=False,
    )
```
